1024 devices in a mesh: dp: 128 (over z, y_hi, x), tensor: 8 (over y_lo, core).
Axes of the slice: x: 4, y: 8 (y_hi: 2, y_lo: 4; y = y_hi * 4 + y_lo), z: 16, core: 2. Of those that a mesh axis runs over, the one named last changes fastest.
Arguments:
- panel: bfloat16 [131072, 3072], P(('dp', 'tensor')), may hold values from -6 to 6
- row_scale: bfloat16 [131072], P(('dp', 'tensor')), may hold values from 0.29882812 to 3
- expert_ids: int32 [131072, 4], P(('dp', 'tensor')), may hold values from 0 to 15, as said below
- weight: bfloat16 [3072, 5376], P('dp', 'tensor'), may hold values from -0.109375 to 0.109375
- up_branch: bfloat16 [49152, 5376], P('dp', 'tensor'), may hold values from -6 to 6
- cotangent: bfloat16 [49152, 5376], P('dp', 'tensor'), may hold values from -6 to 6
Outputs:
- hidden: bfloat16 [49152, 5376], P('dp', 'tensor')
- input_grad: bfloat16 [131072, 3072], P(('dp', 'tensor'))
The draws below stay inside these ranges and needn't reach their ends.
Inputs may be any that keep to these rules, and one draw needn't show every extreme that they name: `expert_ids`: each row names 4 different experts. Among the 128 rows of one device at most 48 name expert 0, and in every draw some device has exactly 48.
All inputs are finite; a program needn't handle non-finite values.
Results may differ from the reference program's by a relative error of at most 0.017.
Values may be sent and summed in bfloat16 or wider, within the bound.
No kernel may reach another device: no remote copies, remote signals or barrier semaphores. Data moves between devices by JAX's collectives and lax.ppermute only.
A program may use at most 32 MiB of HBM per device.

```python
import math
import jax
import jax.numpy as jnp
from jax import lax

D = 3072
FF = 5376
EXPERTS = 16
TOP = 4
TOK_DEV = 128
MOST = 48
TOKENS = 131072
SLOTS = 49152
N_TENSOR = 8


def draw_expert_ids(key, part):
    key = jax.random.fold_in(key, 11)
    keys = jax.random.split(key, 5)
    ndev = TOKENS // TOK_DEV
    counts = jax.random.randint(keys[0], (ndev,), MOST // 3, MOST + 1)
    peak = jax.random.randint(keys[1], (), 0, ndev)
    counts = jnp.where(jnp.arange(ndev) == peak, MOST, counts)
    scores = jax.random.randint(keys[2], (ndev, TOK_DEV), 0, 2 ** 20) * TOK_DEV + jnp.arange(TOK_DEV)[None, :]
    ranks = jnp.argsort(jnp.argsort(scores, axis=1), axis=1)
    chosen = (ranks < counts[:, None]).reshape(TOKENS)
    others = jax.random.randint(keys[3], (TOKENS, EXPERTS - 1), 0, 2 ** 20) * (EXPERTS - 1) + jnp.arange(EXPERTS - 1)[None, :]
    picks = jnp.argsort(others, axis=1)[:, :TOP] + 1
    column = jax.random.randint(keys[4], (TOKENS,), 0, TOP)
    place = chosen[:, None] & (jnp.arange(TOP)[None, :] == column[:, None])
    return jnp.where(place, 0, picks).astype(jnp.int32)


def shard_levels(key, shape, pieces, least, top_value):
    def one(position, blocks):
        draws = jax.random.uniform(jax.random.fold_in(jax.random.fold_in(key, 6), position), (blocks,), jnp.float32, least / len(pieces), top_value / len(pieces))
        return jnp.repeat(jnp.exp(draws), shape[position] // blocks).reshape((-1,) + (1,) * (len(shape) - position - 1))

    gain = one(*pieces[0])
    for cut in pieces[1:]:
        gain = gain * one(*cut)
    return gain


def scatter_about(rng, shape, scale, limit, cuts=(), held_as=jnp.bfloat16):
    gain = shard_levels(rng, shape, cuts, -0.22, 0.18) if cuts else 1.0
    entries = jax.random.normal(rng, shape, jnp.float32) * scale * gain
    return jnp.minimum(jnp.maximum(entries, -limit), limit).astype(held_as)


def setup_inputs(seed: int = 0) -> dict:
    key_of = jax.random.split(jax.random.key(seed), 7)
    panel = scatter_about(key_of[0], (TOKENS, D), 1.0, 6.0, ((0, 1024),))
    row_scale = jnp.clip(jnp.exp(math.log(3.0) - 2.306499 * jax.random.uniform(key_of[1], (TOKENS,), jnp.float32) ** shard_levels(key_of[1], (TOKENS,), ((0, 1024),), -0.2, 0.2)), 0.29882812, 3.0).astype(jnp.bfloat16)
    expert_ids = draw_expert_ids(jax.random.fold_in(key_of[6], 71), 0)
    weight = scatter_about(key_of[3], (D, FF), D ** -0.5, 0.109375, ((0, 128), (1, 8)))
    up_branch = scatter_about(key_of[4], (SLOTS, FF), 1.0, 6.0, ((0, 128), (1, 8)))
    cotangent = scatter_about(key_of[5], (SLOTS, FF), 1.0, 6.0, ((0, 128), (1, 8)))
    return dict(panel=panel, row_scale=row_scale, expert_ids=expert_ids, weight=weight, up_branch=up_branch, cotangent=cotangent)


def reference(panel, row_scale, expert_ids, weight, up_branch, cotangent):
    ndev = TOKENS // TOK_DEV
    groups = ndev // N_TENSOR
    width = FF // N_TENSOR
    hit = jnp.any(expert_ids == 0, axis=1).reshape(ndev, TOK_DEV)
    place = jnp.cumsum(hit.astype(jnp.int32), axis=1) - 1
    slots = jnp.arange(MOST, dtype=jnp.int32)
    match = (place[:, None, :] == slots[None, :, None]) & hit[:, None, :]
    positions = jnp.arange(TOK_DEV, dtype=jnp.int32)
    source = jnp.sum(jnp.where(match, positions[None, None, :], 0), axis=2).astype(jnp.int32)
    valid = jnp.any(match, axis=2)
    flat_source = (source + (jnp.arange(ndev, dtype=jnp.int32) * TOK_DEV)[:, None]).reshape(groups, N_TENSOR * MOST)
    flat_valid = valid.reshape(groups, N_TENSOR * MOST)
    up_groups = up_branch.reshape(groups, N_TENSOR * MOST, FF)
    cot_groups = cotangent.reshape(groups, N_TENSOR * MOST, FF)

    def one_group(items):
        index, keep, upper, cot = items
        rows = jnp.where(keep[:, None], jnp.take(panel, index, axis=0), jnp.zeros((), jnp.bfloat16))
        scales = jnp.where(keep, jnp.take(row_scale, index, axis=0), jnp.zeros((), jnp.bfloat16))
        gate = jnp.dot(rows, weight, preferred_element_type=jnp.float32) * scales.astype(jnp.float32)[:, None]
        sig = jax.nn.sigmoid(gate)
        upper32 = upper.astype(jnp.float32)
        hidden = (gate * sig * upper32).astype(jnp.bfloat16)
        dgate = jnp.where(keep[:, None], cot.astype(jnp.float32) * upper32 * sig * (1.0 + gate * (1.0 - sig)), jnp.zeros((), jnp.float32)).astype(jnp.bfloat16)
        total = jnp.zeros((N_TENSOR * MOST, D), jnp.float32)
        for part in range(N_TENSOR):
            term = jnp.dot(dgate[:, part * width:(part + 1) * width], weight[:, part * width:(part + 1) * width].T, preferred_element_type=jnp.float32).astype(jnp.bfloat16)
            term = lax.optimization_barrier(term)
            total = total + term.astype(jnp.float32)
        return hidden, total.astype(jnp.bfloat16)

    hidden, slot_grad = lax.map(one_group, (flat_source, flat_valid, up_groups, cot_groups))
    hidden = hidden.reshape(SLOTS, FF)
    slot_grad = slot_grad.reshape(ndev, MOST, D)
    target = jnp.where(valid, source, TOK_DEV).astype(jnp.int32)
    devices = jnp.arange(ndev, dtype=jnp.int32)[:, None]
    input_grad = jnp.zeros((ndev, TOK_DEV, D), jnp.bfloat16).at[devices, target].set(slot_grad, mode="drop")
    return hidden, input_grad.reshape(TOKENS, D)
```

```python
import jax
import jax.numpy as jnp
from jax import lax
from jax.sharding import Mesh, PartitionSpec as P

AXES = ("za", "zb", "yh", "x", "yl", "core")
SIZES = (4, 4, 2, 4, 4, 2)
GROUP = ("za", "zb", "yh", "x")
TENSOR = ("yl", "core")


def shifted(za, zb, by):
    count = za * zb
    return [(i, (i + by) % count) for i in range(count)]


def everyone(part, axes):
    count = lax.axis_size(axes)
    return lax.all_to_all(jnp.broadcast_to(part[None], (count,) + part.shape), axes, 0, 0)


def z_neighbours(part):
    za, zb = lax.axis_size("za"), lax.axis_size("zb")
    return [lax.ppermute(part, ("za", "zb"), shifted(za, zb, by)) for by in (1, -1, -2)]


def by_residue(own, others):
    below, above, far = others
    zb = lax.axis_index("zb")
    out = []
    for r in range(4):
        away = (r - zb) % 4
        out.append(
            jnp.where(away == 0, own, jnp.where(away == 1, above, jnp.where(away == 2, far, below)))
        )
    return jnp.stack(out)


def body(panel, row_scale, expert_ids, weight, up_branch, cotangent):
    n_yl, n_core = lax.axis_size("yl"), lax.axis_size("core")
    slot_count = up_branch.shape[0] // (n_yl * n_core)
    depth, width = weight.shape
    model = panel.shape[1]
    cut = (width // 2 + 127) // 128 * 128

    hit = jnp.any(expert_ids == 0, axis=1)
    place = jnp.cumsum(hit.astype(jnp.int32)) - 1
    slots = jnp.arange(slot_count, dtype=jnp.int32)
    select = ((place[None, :] == slots[:, None]) & hit[None, :]).astype(jnp.bfloat16)
    own_rows = jnp.dot(select, panel, preferred_element_type=jnp.float32).astype(jnp.bfloat16)
    own_scale = jnp.dot(
        select, jnp.broadcast_to(row_scale[:, None], (row_scale.shape[0], 128)),
        preferred_element_type=jnp.float32,
    ).astype(jnp.bfloat16)
    sent = jnp.concatenate([own_rows, own_scale], axis=1)
    got = lax.all_gather(sent, TENSOR, axis=0, tiled=True)
    rows = got[:, :model]
    scales32 = got[:, model:model + 1].astype(jnp.float32)

    far = everyone(weight, ("za", "yh")).reshape(4, 2, depth, width)
    one, two = far[..., :cut], far[..., cut:]
    one_z = by_residue(one, z_neighbours(one))
    two_x = everyone(two, ("x",))
    two_z = z_neighbours(two_x)
    one_x = everyone(one_z, ("x",))
    w_one = one_x.transpose(2, 1, 3, 0, 4, 5).reshape(model, cut)
    w_two = by_residue(two_x, two_z).transpose(2, 0, 3, 1, 4, 5).reshape(model, width - cut)
    gathered = jnp.concatenate([w_one, w_two], axis=1)

    product = jnp.dot(rows, gathered, preferred_element_type=jnp.float32)
    gate = product * scales32
    sig = jax.nn.sigmoid(gate)
    upper = up_branch.astype(jnp.float32)
    hidden = (gate * sig * upper).astype(jnp.bfloat16)
    filled = scales32 > 0.0
    dgate = jnp.where(
        filled,
        cotangent.astype(jnp.float32) * upper * sig * (1.0 + gate * (1.0 - sig)),
        0.0,
    ).astype(jnp.bfloat16)

    core = lax.axis_index("core")
    halves = dgate.reshape(n_yl, n_core, slot_count, width)

    def back(which):
        part = lax.dynamic_index_in_dim(halves, which, 1, keepdims=False)
        part = part.reshape(n_yl * slot_count, width)
        return jnp.dot(part, gathered.T, preferred_element_type=jnp.float32).astype(jnp.bfloat16)

    swapped = lax.ppermute(back(1 - core), "core", [(0, 1), (1, 0)])
    pair = (back(core).astype(jnp.float32) + swapped.astype(jnp.float32)).astype(jnp.bfloat16)
    parts = lax.all_to_all(pair.reshape(n_yl, slot_count, model), "yl", 0, 0)
    slot_grad = jnp.sum(parts.astype(jnp.float32), axis=0).astype(jnp.bfloat16)
    input_grad = jnp.einsum(
        "st,sd->td", select, slot_grad, preferred_element_type=jnp.float32
    ).astype(jnp.bfloat16)
    return (hidden, input_grad)


def solution(mesh):
    fine = Mesh(mesh.devices.reshape(SIZES), AXES)
    in_specs = (
        P(AXES, None),
        P(AXES),
        P(AXES, None),
        P(GROUP, TENSOR),
        P(GROUP, TENSOR),
        P(GROUP, TENSOR),
    )
    out_specs = (P(GROUP, TENSOR), P(AXES, None))
    return jax.shard_map(body, mesh=fine, in_specs=in_specs, out_specs=out_specs, check_vma=False)
```

```python
import jax
import jax.numpy as jnp
from jax import lax
from jax.sharding import Mesh, PartitionSpec as P

AXES = ("za", "zb", "yh", "x", "yl", "core")
SIZES = (4, 4, 2, 4, 4, 2)
GROUP = ("za", "zb", "yh", "x")
TENSOR = ("yl", "core")


def shifted(za, zb, by):
    count = za * zb
    return [(i, (i + by) % count) for i in range(count)]


def everyone(part, axes):
    count = lax.axis_size(axes)
    return lax.all_to_all(jnp.broadcast_to(part[None], (count,) + part.shape), axes, 0, 0)


def along_z(part, by):
    za, zb = lax.axis_size("za"), lax.axis_size("zb")
    return lax.ppermute(part, ("za", "zb"), shifted(za, zb, by))


def in_order(own, other, which):
    return jnp.where(which == 0, jnp.stack([own, other]), jnp.stack([other, own]))


def by_residue(own, below, above, far):
    zb = lax.axis_index("zb")
    out = []
    for r in range(4):
        away = (r - zb) % 4
        out.append(
            jnp.where(away == 0, own, jnp.where(away == 1, above, jnp.where(away == 2, far, below)))
        )
    return jnp.stack(out)


def body(panel, row_scale, expert_ids, weight, up_branch, cotangent):
    n_yl, n_core = lax.axis_size("yl"), lax.axis_size("core")
    slot_count = up_branch.shape[0] // (n_yl * n_core)
    depth, width = weight.shape
    model = panel.shape[1]
    cut = (width // 2 + 127) // 128 * 128

    hit = jnp.any(expert_ids == 0, axis=1)
    place = jnp.cumsum(hit.astype(jnp.int32)) - 1
    slots = jnp.arange(slot_count, dtype=jnp.int32)
    select = ((place[None, :] == slots[:, None]) & hit[None, :]).astype(jnp.bfloat16)
    own_rows = jnp.dot(select, panel, preferred_element_type=jnp.float32).astype(jnp.bfloat16)
    own_scale = jnp.dot(
        select, jnp.broadcast_to(row_scale[:, None], (row_scale.shape[0], 128)),
        preferred_element_type=jnp.float32,
    ).astype(jnp.bfloat16)
    sent = jnp.concatenate([own_rows, own_scale], axis=1)
    core = lax.axis_index("core")

    far = everyone(weight, ("za", "yh")).reshape(4, 2, depth, width)
    far, sent = lax.optimization_barrier((far, sent))

    one, two = far[..., :cut], far[..., cut:]
    one_z = by_residue(one, along_z(one, 1), along_z(one, -1), along_z(one, -2))
    two_x = everyone(two, ("x",))
    zb = lax.axis_index("zb")
    two_far = jnp.concatenate([along_z(two_x[:2], -2), along_z(two_x[2:], 2)])
    one_x = everyone(one_z, ("x",))

    near = lax.ppermute(sent, "yl", [(i, i ^ 1) for i in range(4)])
    yl = lax.axis_index("yl")
    two_rows = in_order(sent, near, yl % 2)
    other_rows = lax.ppermute(two_rows, "yl", [(i, i ^ 2) for i in range(4)])
    four_rows = in_order(two_rows, other_rows, yl // 2)
    four_rows = four_rows.reshape(n_yl, slot_count, model + 128)
    theirs = lax.ppermute(four_rows, "core", [(0, 1), (1, 0)])
    got = jnp.where(core == 0, jnp.stack([four_rows, theirs], 1), jnp.stack([theirs, four_rows], 1))
    got = got.reshape(n_yl * n_core * slot_count, model + 128)
    rows = got[:, :model]
    scales32 = got[:, model:model + 1].astype(jnp.float32)

    whole = jnp.zeros((4, 4, 2, 4, depth, width), jnp.bfloat16)
    zero = jnp.zeros((), jnp.int32)
    for piece, by in ((two_x, 0), (along_z(two_x, 1), -1), (along_z(two_x, -1), 1), (two_far, 2)):
        piece = piece.transpose(1, 2, 0, 3, 4)[:, None]
        at = (zero, (zb + by + 4) % 4, zero, zero, zero, zero + cut)
        whole = lax.dynamic_update_slice(whole, piece, at)
    whole = whole.at[..., :cut].set(one_x.transpose(2, 1, 3, 0, 4, 5))
    gathered = whole.reshape(model, width)

    product = jnp.dot(rows, gathered, preferred_element_type=jnp.float32)
    gate = product * scales32
    sig = jax.nn.sigmoid(gate)
    upper = up_branch.astype(jnp.float32)
    hidden = (gate * sig * upper).astype(jnp.bfloat16)
    filled = scales32 > 0.0
    dgate = jnp.where(
        filled,
        cotangent.astype(jnp.float32) * upper * sig * (1.0 + gate * (1.0 - sig)),
        0.0,
    ).astype(jnp.bfloat16)

    partial = jnp.dot(dgate, gathered.T, preferred_element_type=jnp.float32).astype(jnp.bfloat16)
    partial = partial.reshape(n_yl, n_core, slot_count, model)
    given = lax.dynamic_index_in_dim(partial, 1 - core, 1, keepdims=False)
    kept = lax.dynamic_index_in_dim(partial, core, 1, keepdims=False)
    swapped = lax.ppermute(given, "core", [(0, 1), (1, 0)])
    pair = (kept.astype(jnp.float32) + swapped.astype(jnp.float32)).astype(jnp.bfloat16)
    parts = lax.all_to_all(pair, "yl", 0, 0)
    slot_grad = jnp.sum(parts.astype(jnp.float32), axis=0).astype(jnp.bfloat16)
    input_grad = jnp.einsum(
        "st,sd->td", select, slot_grad, preferred_element_type=jnp.float32
    ).astype(jnp.bfloat16)
    return (hidden, input_grad)


def solution(mesh):
    fine = Mesh(mesh.devices.reshape(SIZES), AXES)
    in_specs = (
        P(AXES, None),
        P(AXES),
        P(AXES, None),
        P(GROUP, TENSOR),
        P(GROUP, TENSOR),
        P(GROUP, TENSOR),
    )
    out_specs = (P(GROUP, TENSOR), P(AXES, None))
    return jax.shard_map(body, mesh=fine, in_specs=in_specs, out_specs=out_specs, check_vma=False)
```

```python
import jax
import jax.numpy as jnp
from jax import lax
from jax.sharding import Mesh, PartitionSpec as P

AXES = ("za", "zb", "yh", "x", "yl", "core")
SIZES = (4, 4, 2, 4, 4, 2)
GROUP = ("za", "zb", "yh", "x")
TENSOR = ("yl", "core")


def shifted(za, zb, by):
    count = za * zb
    return [(i, (i + by) % count) for i in range(count)]


def everyone(part, axes):
    count = lax.axis_size(axes)
    return lax.all_to_all(jnp.broadcast_to(part[None], (count,) + part.shape), axes, 0, 0)


def along_z(part, by):
    za, zb = lax.axis_size("za"), lax.axis_size("zb")
    return lax.ppermute(part, ("za", "zb"), shifted(za, zb, by))


def in_order(own, other, which):
    return jnp.where(which == 0, jnp.stack([own, other]), jnp.stack([other, own]))


def nothing(array):
    return (array[(0,) * array.ndim] * 0).astype(jnp.int32)


def by_residue(own, below, above, far):
    zb = lax.axis_index("zb")
    out = []
    for r in range(4):
        away = (r - zb) % 4
        out.append(
            jnp.where(away == 0, own, jnp.where(away == 1, above, jnp.where(away == 2, far, below)))
        )
    return jnp.stack(out)


def body(panel, row_scale, expert_ids, weight, up_branch, cotangent):
    n_yl, n_core = lax.axis_size("yl"), lax.axis_size("core")
    slot_count = up_branch.shape[0] // (n_yl * n_core)
    depth, width = weight.shape
    model = panel.shape[1]
    cut = (width // 2 + 127) // 128 * 128

    hit = jnp.any(expert_ids == 0, axis=1)
    place = jnp.cumsum(hit.astype(jnp.int32)) - 1
    slots = jnp.arange(slot_count, dtype=jnp.int32)
    select = ((place[None, :] == slots[:, None]) & hit[None, :]).astype(jnp.bfloat16)
    own_rows = jnp.dot(select, panel, preferred_element_type=jnp.float32).astype(jnp.bfloat16)
    own_scale = jnp.dot(
        select, jnp.broadcast_to(row_scale[:, None], (row_scale.shape[0], 128)),
        preferred_element_type=jnp.float32,
    ).astype(jnp.bfloat16)
    sent = jnp.concatenate([own_rows, own_scale], axis=1)
    core = lax.axis_index("core")

    yl = lax.axis_index("yl")
    by_one, by_two = [(i, i ^ 1) for i in range(4)], [(i, i ^ 2) for i in range(4)]
    near = lax.ppermute(sent, "yl", by_one)
    opposite = lax.ppermute(sent, "yl", by_two)

    far = everyone(weight, ("za", "yh")).reshape(4, 2, depth, width)
    one, two = far[..., :cut], far[..., cut:]
    last = lax.ppermute(near, "yl", by_two)
    two_x = everyone(two, ("x",))
    beside = (along_z(one, 1), along_z(one, -1), along_z(one, -2))
    one_x = everyone(by_residue(one, *beside), ("x",))
    zb = lax.axis_index("zb")
    out = []
    for r in range(4):
        away = (r - zb) % 4
        out.append(
            jnp.where(away == 0, own, jnp.where(away == 1, above, jnp.where(away == 2, far, below)))
        )
    return jnp.stack(out)


def body(panel, row_scale, expert_ids, weight, up_branch, cotangent):
    n_yl, n_core = lax.axis_size("yl"), lax.axis_size("core")
    slot_count = up_branch.shape[0] // (n_yl * n_core)
    depth, width = weight.shape
    model = panel.shape[1]
    cut = (width // 2 + 127) // 128 * 128

    hit = jnp.any(expert_ids == 0, axis=1)
    place = jnp.cumsum(hit.astype(jnp.int32)) - 1
    slots = jnp.arange(slot_count, dtype=jnp.int32)
    select = ((place[None, :] == slots[:, None]) & hit[None, :]).astype(jnp.bfloat16)
    own_rows = jnp.dot(select, panel, preferred_element_type=jnp.float32).astype(jnp.bfloat16)
    own_scale = jnp.dot(
        select, jnp.broadcast_to(row_scale[:, None], (row_scale.shape[0], 128)),
        preferred_element_type=jnp.float32,
    ).astype(jnp.bfloat16)
    sent = jnp.concatenate([own_rows, own_scale], axis=1)
    core = lax.axis_index("core")

    yl = lax.axis_index("yl")
    by_one, by_two = [(i, i ^ 1) for i in range(4)], [(i, i ^ 2) for i in range(4)]
    near = lax.ppermute(sent, "yl", by_one)
    opposite = lax.ppermute(sent, "yl", by_two)

    far = everyone(weight, ("za", "yh")).reshape(4, 2, depth, width)
    one, two = far[..., :cut], far[..., cut:]
    last = lax.ppermute(near, "yl", by_two)
    two_x = everyone(two, ("x",))
    beside = (along_z(one, 1), along_z(one, -1), along_z(one, -2))
    one_x = everyone(by_residue(one, *beside), ("x",))
    four_rows = in_order(in_order(sent, near, yl % 2), in_order(opposite, last, yl % 2), yl // 2)
    four_rows = four_rows.reshape(n_yl, slot_count, model + 128)
    theirs = lax.ppermute(four_rows, "core", [(0, 1), (1, 0)])
    zb = lax.axis_index("zb")
    two_far = jnp.concatenate([along_z(two_x[:2], -2), along_z(two_x[2:], 2)])

    below, above = along_z(two_x, 1), along_z(two_x, -1)
    below, last = lax.optimization_barrier((below, last))
    first = core + nothing(above) == 0
    got = jnp.where(first, jnp.stack([four_rows, theirs], 1), jnp.stack([theirs, four_rows], 1))
    got = got.reshape(n_yl * n_core * slot_count, model + 128)
    rows = got[:, :model]
    scales32 = got[:, model:model + 1].astype(jnp.float32)

    whole = jnp.zeros((4, 4, 2, 4, depth, width), jnp.bfloat16)
    zero = jnp.zeros((), jnp.int32)
    for piece, by in ((two_x, 0), (below, -1), (above, 1), (two_far, 2)):
        piece = piece.transpose(1, 2, 0, 3, 4)[:, None]
        at = (zero, (zb + by + 4) % 4, zero, zero, zero, zero + cut)
        whole = lax.dynamic_update_slice(whole, piece, at)
    whole = whole.at[..., :cut].set(one_x.transpose(2, 1, 3, 0, 4, 5))
    gathered = whole.reshape(model, width)

    product = jnp.dot(rows, gathered, preferred_element_type=jnp.float32)
    gate = product * scales32
    sig = jax.nn.sigmoid(gate)
    upper = up_branch.astype(jnp.float32)
    hidden = (gate * sig * upper).astype(jnp.bfloat16)
    filled = scales32 > 0.0
    dgate = jnp.where(
        filled,
        cotangent.astype(jnp.float32) * upper * sig * (1.0 + gate * (1.0 - sig)),
        0.0,
    ).astype(jnp.bfloat16)

    def pick(array, axis, which):
        return lax.dynamic_index_in_dim(array, which, axis, keepdims=False)

    def add(one, other):
        return (one.astype(jnp.float32) + other.astype(jnp.float32)).astype(jnp.bfloat16)

    partial = jnp.dot(dgate, gathered.T, preferred_element_type=jnp.float32).astype(jnp.bfloat16)
    partial = partial.reshape(2, 2, n_core, slot_count, model)

    def returned(part):
        swapped = lax.ppermute(pick(part, 2, 1 - core), "core", [(0, 1), (1, 0)])
        pair = add(pick(part, 2, core), swapped)
        near = lax.ppermute(pick(pair, 1, 1 - yl % 2), "yl", by_one)
        four = add(pick(pair, 1, yl % 2), near)
        far = lax.ppermute(pick(four, 0, 1 - yl // 2), "yl", by_two)
        return add(pick(four, 0, yl // 2), far)

    half = model // 2
    slot_grad = jnp.concatenate([returned(partial[..., :half]), returned(partial[..., half:])], axis=1)
    input_grad = jnp.einsum(
        "st,sd->td", select, slot_grad, preferred_element_type=jnp.float32
    ).astype(jnp.bfloat16)
    return (hidden, input_grad)


def solution(mesh):
    fine = Mesh(mesh.devices.reshape(SIZES), AXES)
    in_specs = (
        P(AXES, None),
        P(AXES),
        P(AXES, None),
        P(GROUP, TENSOR),
        P(GROUP, TENSOR),
        P(GROUP, TENSOR),
    )
    out_specs = (P(GROUP, TENSOR), P(AXES, None))
    return jax.shard_map(body, mesh=fine, in_specs=in_specs, out_specs=out_specs, check_vma=False)
```

```python
import jax
import jax.numpy as jnp
from jax import lax
from jax.sharding import Mesh, PartitionSpec as P

AXES = ("za", "zb", "yh", "x", "yl", "core")
SIZES = (4, 4, 2, 4, 4, 2)
GROUP = ("za", "zb", "yh", "x")
TENSOR = ("yl", "core")


def shifted(za, zb, by):
    count = za * zb
    return [(i, (i + by) % count) for i in range(count)]


def everyone(part, axes):
    count = lax.axis_size(axes)
    return lax.all_to_all(jnp.broadcast_to(part[None], (count,) + part.shape), axes, 0, 0)


def along_z(part, by):
    za, zb = lax.axis_size("za"), lax.axis_size("zb")
    return lax.ppermute(part, ("za", "zb"), shifted(za, zb, by))


def in_order(own, other, which):
    return jnp.where(which == 0, jnp.stack([own, other]), jnp.stack([other, own]))


def nothing(array):
    return (array[(0,) * array.ndim] * 0).astype(jnp.int32)


def by_residue(own, below, above, far):
    zb = lax.axis_index("zb")
    out = []
    for r in range(4):
        away = (r - zb) % 4
        out.append(
            jnp.where(away == 0, own, jnp.where(away == 1, above, jnp.where(away == 2, far, below)))
        )
    return jnp.stack(out)


def body(panel, row_scale, expert_ids, weight, up_branch, cotangent):
    n_yl, n_core = lax.axis_size("yl"), lax.axis_size("core")
    slot_count = up_branch.shape[0] // (n_yl * n_core)
    depth, width = weight.shape
    model = panel.shape[1]
    cut = (width // 2 + 127) // 128 * 128

    hit = jnp.any(expert_ids == 0, axis=1)
    place = jnp.cumsum(hit.astype(jnp.int32)) - 1
    slots = jnp.arange(slot_count, dtype=jnp.int32)
    select = ((place[None, :] == slots[:, None]) & hit[None, :]).astype(jnp.bfloat16)
    own_rows = jnp.dot(select, panel, preferred_element_type=jnp.float32).astype(jnp.bfloat16)
    own_scale = jnp.dot(
        select, jnp.broadcast_to(row_scale[:, None], (row_scale.shape[0], 128)),
        preferred_element_type=jnp.float32,
    ).astype(jnp.bfloat16)
    sent = jnp.concatenate([own_rows, own_scale], axis=1)
    core = lax.axis_index("core")

    yl = lax.axis_index("yl")
    by_one, by_two = [(i, i ^ 1) for i in range(4)], [(i, i ^ 2) for i in range(4)]
    near = lax.ppermute(sent, "yl", by_one)

    far = everyone(weight, ("za", "yh")).reshape(4, 2, depth, width)
    far, near = lax.optimization_barrier((far, near))
    one, two = far[..., :cut], far[..., cut:]
    beside = (along_z(one, 1), along_z(one, -1), along_z(one, -2))
    two_rows = in_order(sent, near, (yl + nothing(beside[2])) % 2)
    opposite = lax.ppermute(two_rows, "yl", by_two)
    one_x = everyone(by_residue(one, *beside), ("x",))
    two_x = everyone(two, ("x",))
    zb = lax.axis_index("zb")
    below, above = along_z(two_x, 1), along_z(two_x, -1)
    two_far = jnp.concatenate([along_z(two_x[:2], -2), along_z(two_x[2:], 2)])

    four_rows = in_order(two_rows, opposite, yl // 2)
    four_rows = four_rows.reshape(n_yl, slot_count, model + 128)
    theirs = lax.ppermute(four_rows, "core", [(0, 1), (1, 0)])
    got = jnp.where(core == 0, jnp.stack([four_rows, theirs], 1), jnp.stack([theirs, four_rows], 1))
    got = got.reshape(n_yl * n_core * slot_count, model + 128)
    rows = got[:, :model]
    scales32 = got[:, model:model + 1].astype(jnp.float32)

    whole = jnp.zeros((4, 4, 2, 4, depth, width), jnp.bfloat16)
    zero = jnp.zeros((), jnp.int32)

    def placed(whole, piece, by, after):
        piece = piece.transpose(1, 2, 0, 3, 4)[:, None]
        at = (zero, (zb + by + after) % 4, zero, zero, zero, zero + cut)
        return lax.dynamic_update_slice(whole, piece, at)

    whole = placed(whole, two_x, 0, 4)
    whole = placed(whole, below, -1, 4)
    whole = placed(whole, above, 1, 4)
    whole = whole.at[..., :cut].set(one_x.transpose(2, 1, 3, 0, 4, 5))
    whole = placed(whole, two_far, 2, 4)
    gathered = whole.reshape(model, width)

    product = jnp.dot(rows, gathered, preferred_element_type=jnp.float32)
    gate = product * scales32
    sig = jax.nn.sigmoid(gate)
    upper = up_branch.astype(jnp.float32)
    hidden = (gate * sig * upper).astype(jnp.bfloat16)
    filled = scales32 > 0.0
    dgate = jnp.where(
        filled,
        cotangent.astype(jnp.float32) * upper * sig * (1.0 + gate * (1.0 - sig)),
        0.0,
    ).astype(jnp.bfloat16)

    def pick(array, axis, which):
        return lax.dynamic_index_in_dim(array, which, axis, keepdims=False)

    def add(one, other):
        return (one.astype(jnp.float32) + other.astype(jnp.float32)).astype(jnp.bfloat16)

    partial = jnp.dot(dgate, gathered.T, preferred_element_type=jnp.float32).astype(jnp.bfloat16)
    partial = partial.reshape(2, 2, n_core, slot_count, model)

    def returned(part):
        swapped = lax.ppermute(pick(part, 2, 1 - core), "core", [(0, 1), (1, 0)])
        pair = add(pick(part, 2, core), swapped)
        near = lax.ppermute(pick(pair, 1, 1 - yl % 2), "yl", by_one)
        four = add(pick(pair, 1, yl % 2), near)
        far = lax.ppermute(pick(four, 0, 1 - yl // 2), "yl", by_two)
        return add(pick(four, 0, yl // 2), far)

    half = model // 2
    slot_grad = jnp.concatenate([returned(partial[..., :half]), returned(partial[..., half:])], axis=1)
    input_grad = jnp.einsum(
        "st,sd->td", select, slot_grad, preferred_element_type=jnp.float32
    ).astype(jnp.bfloat16)
    return (hidden, input_grad)


def solution(mesh):
    fine = Mesh(mesh.devices.reshape(SIZES), AXES)
    in_specs = (
        P(AXES, None),
        P(AXES),
        P(AXES, None),
        P(GROUP, TENSOR),
        P(GROUP, TENSOR),
        P(GROUP, TENSOR),
    )
    out_specs = (P(GROUP, TENSOR), P(AXES, None))
    return jax.shard_map(body, mesh=fine, in_specs=in_specs, out_specs=out_specs, check_vma=False)
```

```python
import jax
import jax.numpy as jnp
from jax import lax
from jax.sharding import Mesh, PartitionSpec as P

AXES = ("za", "zb", "yh", "x", "yl", "core")
SIZES = (4, 4, 2, 4, 4, 2)
GROUP = ("za", "zb", "yh", "x")
TENSOR = ("yl", "core")


def shifted(za, zb, by):
    count = za * zb
    return [(i, (i + by) % count) for i in range(count)]


def everyone(part, axes):
    count = lax.axis_size(axes)
    return lax.all_to_all(jnp.broadcast_to(part[None], (count,) + part.shape), axes, 0, 0)


def along_z(part, by):
    za, zb = lax.axis_size("za"), lax.axis_size("zb")
    return lax.ppermute(part, ("za", "zb"), shifted(za, zb, by))


def two_along_z(part):
    za, zb, core = lax.axis_size("za"), lax.axis_size("zb"), lax.axis_size("core")
    count = za * zb
    pairs = []
    for z in range(count):
        for c in range(core):
            pairs.append((z * core + c, (z + (2 if c else -2)) % count * core + c))
    return lax.ppermute(part, ("za", "zb", "core"), pairs)


def in_order(own, other, which):
    return jnp.where(which == 0, jnp.stack([own, other]), jnp.stack([other, own]))


def nothing(array):
    return (array[(0,) * array.ndim] * 0).astype(jnp.int32)


def by_residue(own, below, above, far):
    zb = lax.axis_index("zb")
    out = []
    for r in range(4):
        away = (r - zb) % 4
        out.append(
            jnp.where(away == 0, own, jnp.where(away == 1, above, jnp.where(away == 2, far, below)))
        )
    return jnp.stack(out)


def body(panel, row_scale, expert_ids, weight, up_branch, cotangent):
    n_yl, n_core = lax.axis_size("yl"), lax.axis_size("core")
    slot_count = up_branch.shape[0] // (n_yl * n_core)
    depth, width = weight.shape
    model = panel.shape[1]
    cut = (width // 2 + 127) // 128 * 128

    hit = jnp.any(expert_ids == 0, axis=1)
    place = jnp.cumsum(hit.astype(jnp.int32)) - 1
    slots = jnp.arange(slot_count, dtype=jnp.int32)
    select = ((place[None, :] == slots[:, None]) & hit[None, :]).astype(jnp.bfloat16)
    own_rows = jnp.dot(select, panel, preferred_element_type=jnp.float32).astype(jnp.bfloat16)
    own_scale = jnp.dot(
        select, jnp.broadcast_to(row_scale[:, None], (row_scale.shape[0], 128)),
        preferred_element_type=jnp.float32,
    ).astype(jnp.bfloat16)
    sent = jnp.concatenate([own_rows, own_scale], axis=1)
    core = lax.axis_index("core")

    yl = lax.axis_index("yl")
    by_one, by_two = [(i, i ^ 1) for i in range(4)], [(i, i ^ 2) for i in range(4)]
    near = lax.ppermute(sent, "yl", by_one)

    far = everyone(weight, ("za", "yh")).reshape(4, 2, depth, width)
    far, near = lax.optimization_barrier((far, near))
    one, two = far[..., :cut], far[..., cut:]
    beside = (along_z(one, 1), along_z(one, -1), two_along_z(one))
    two_rows = in_order(sent, near, (yl + nothing(beside[2])) % 2)
    opposite = lax.ppermute(two_rows, "yl", by_two)
    one_x = everyone(by_residue(one, *beside), ("x",))
    two_x = everyone(two, ("x",))
    zb = lax.axis_index("zb")
    below, above = along_z(two_x, 1), along_z(two_x, -1)
    two_far = two_along_z(two_x)

    four_rows = in_order(two_rows, opposite, yl // 2)
    four_rows = four_rows.reshape(n_yl, slot_count, model + 128)
    theirs = lax.ppermute(four_rows, "core", [(0, 1), (1, 0)])
    got = jnp.stack([four_rows, four_rows], 1)
    got = lax.dynamic_update_slice(got, theirs[:, None], (0, 1 - core, 0, 0))
    got = got.reshape(n_yl * n_core * slot_count, model + 128)
    rows = got[:, :model]
    scales32 = got[:, model:model + 1].astype(jnp.float32)

    whole = jnp.zeros((4, 4, 2, 4, depth, width), jnp.bfloat16)
    zero = jnp.zeros((), jnp.int32)

    def placed(whole, piece, by, after):
        piece = piece.transpose(1, 2, 0, 3, 4)[:, None]
        at = (zero, (zb + by + after) % 4, zero, zero, zero, zero + cut)
        return lax.dynamic_update_slice(whole, piece, at)

    whole = placed(whole, two_x, 0, 4)
    whole = placed(whole, below, -1, 4)
    whole = placed(whole, above, 1, 4)
    whole = whole.at[..., :cut].set(one_x.transpose(2, 1, 3, 0, 4, 5))
    whole = placed(whole, two_far, 2, 4)
    gathered = whole.reshape(model, width)

    product = jnp.dot(rows, gathered, preferred_element_type=jnp.float32)
    gate = product * scales32
    sig = jax.nn.sigmoid(gate)
    upper = up_branch.astype(jnp.float32)
    hidden = (gate * sig * upper).astype(jnp.bfloat16)
    filled = scales32 > 0.0
    dgate = jnp.where(
        filled,
        cotangent.astype(jnp.float32) * upper * sig * (1.0 + gate * (1.0 - sig)),
        0.0,
    ).astype(jnp.bfloat16)

    def pick(array, axis, which):
        return lax.dynamic_index_in_dim(array, which, axis, keepdims=False)

    def add(one, other):
        return (one.astype(jnp.float32) + other.astype(jnp.float32)).astype(jnp.bfloat16)

    partial = jnp.dot(dgate, gathered.T, preferred_element_type=jnp.float32).astype(jnp.bfloat16)
    partial = partial.reshape(2, 2, n_core, slot_count, model)

    def returned(part):
        swapped = lax.ppermute(pick(part, 2, 1 - core), "core", [(0, 1), (1, 0)])
        pair = add(pick(part, 2, core), swapped)
        near = lax.ppermute(pick(pair, 1, 1 - yl % 2), "yl", by_one)
        four = add(pick(pair, 1, yl % 2), near)
        far = lax.ppermute(pick(four, 0, 1 - yl // 2), "yl", by_two)
        return add(pick(four, 0, yl // 2), far)

    half = model // 2
    slot_grad = jnp.concatenate([returned(partial[..., :half]), returned(partial[..., half:])], axis=1)
    input_grad = jnp.einsum(
        "st,sd->td", select, slot_grad, preferred_element_type=jnp.float32
    ).astype(jnp.bfloat16)
    return (hidden, input_grad)


def solution(mesh):
    fine = Mesh(mesh.devices.reshape(SIZES), AXES)
    in_specs = (
        P(AXES, None),
        P(AXES),
        P(AXES, None),
        P(GROUP, TENSOR),
        P(GROUP, TENSOR),
        P(GROUP, TENSOR),
    )
    out_specs = (P(GROUP, TENSOR), P(AXES, None))
    return jax.shard_map(body, mesh=fine, in_specs=in_specs, out_specs=out_specs, check_vma=False)
```

```python
import jax
import jax.numpy as jnp
from jax import lax
from jax.sharding import Mesh, PartitionSpec as P

AXES = ("za", "zb", "yh", "x", "yl", "core")
SIZES = (4, 4, 2, 4, 4, 2)
GROUP = ("za", "zb", "yh", "x")
TENSOR = ("yl", "core")


def shifted(za, zb, by):
    count = za * zb
    return [(i, (i + by) % count) for i in range(count)]


def everyone(part, axes):
    count = lax.axis_size(axes)
    return lax.all_to_all(jnp.broadcast_to(part[None], (count,) + part.shape), axes, 0, 0)


def along_z(part, by):
    za, zb = lax.axis_size("za"), lax.axis_size("zb")
    return lax.ppermute(part, ("za", "zb"), shifted(za, zb, by))


def two_along_z(part):
    za, zb, core = lax.axis_size("za"), lax.axis_size("zb"), lax.axis_size("core")
    count = za * zb
    pairs = []
    for z in range(count):
        for c in range(core):
            pairs.append((z * core + c, (z + (2 if c else -2)) % count * core + c))
    return lax.ppermute(part, ("za", "zb", "core"), pairs)


def in_order(own, other, which):
    return jnp.where(which == 0, jnp.stack([own, other]), jnp.stack([other, own]))


def nothing(array):
    return (array[(0,) * array.ndim] * 0).astype(jnp.int32)


def by_residue(own, below, above, far):
    zb = lax.axis_index("zb")
    out = []
    for r in range(4):
        away = (r - zb) % 4
        out.append(
            jnp.where(away == 0, own, jnp.where(away == 1, above, jnp.where(away == 2, far, below)))
        )
    return jnp.stack(out)


def body(panel, row_scale, expert_ids, weight, up_branch, cotangent):
    n_yl, n_core = lax.axis_size("yl"), lax.axis_size("core")
    slot_count = up_branch.shape[0] // (n_yl * n_core)
    depth, width = weight.shape
    model = panel.shape[1]
    cut = (width // 2 + 127) // 128 * 128

    hit = jnp.any(expert_ids == 0, axis=1)
    place = jnp.cumsum(hit.astype(jnp.int32)) - 1
    slots = jnp.arange(slot_count, dtype=jnp.int32)
    select = ((place[None, :] == slots[:, None]) & hit[None, :]).astype(jnp.bfloat16)
    own_rows = jnp.dot(select, panel, preferred_element_type=jnp.float32).astype(jnp.bfloat16)
    own_scale = jnp.dot(
        select, jnp.broadcast_to(row_scale[:, None], (row_scale.shape[0], 128)),
        preferred_element_type=jnp.float32,
    ).astype(jnp.bfloat16)
    sent = jnp.concatenate([own_rows, own_scale], axis=1)
    core = lax.axis_index("core")

    yl = lax.axis_index("yl")
    by_one, by_two = [(i, i ^ 1) for i in range(4)], [(i, i ^ 2) for i in range(4)]
    opposite = lax.ppermute(sent, "yl", by_two)

    far = everyone(weight, ("za", "yh")).reshape(4, 2, depth, width)
    far, opposite = lax.optimization_barrier((far, opposite))
    one, two = far[..., :cut], far[..., cut:]
    beside = (along_z(one, 1), along_z(one, -1), two_along_z(one))
    two_rows = in_order(sent, opposite, (yl + nothing(beside[2])) // 2)
    beyond = lax.ppermute(two_rows, "yl", by_one)
    one_x = everyone(by_residue(one, *beside), ("x",))
    two_x = everyone(two, ("x",))
    zb = lax.axis_index("zb")
    below, above = along_z(two_x, 1), along_z(two_x, -1)
    two_far = two_along_z(two_x)

    def between(even, odd):
        return jnp.concatenate([even[:1], odd[:1], even[1:], odd[1:]])

    four_rows = jnp.where(yl % 2 == 0, between(two_rows, beyond), between(beyond, two_rows))
    theirs = lax.ppermute(four_rows, "core", [(0, 1), (1, 0)])
    got = jnp.stack([four_rows, four_rows], 1)
    got = lax.dynamic_update_slice(got, theirs[:, None], (0, 1 - core, 0, 0))
    got = got.reshape(n_yl * n_core * slot_count, model + 128)
    rows = got[:, :model]
    scales32 = got[:, model:model + 1].astype(jnp.float32)

    whole = jnp.zeros((4, 4, 2, 4, depth, width), jnp.bfloat16)
    zero = jnp.zeros((), jnp.int32)

    def placed(whole, piece, by, after):
        piece = piece.transpose(1, 2, 0, 3, 4)[:, None]
        at = (zero, (zb + by + after) % 4, zero, zero, zero, zero + cut)
        return lax.dynamic_update_slice(whole, piece, at)

    whole = placed(whole, two_x, 0, 4)
    whole = placed(whole, below, -1, 4)
    whole = placed(whole, above, 1, 4)
    whole = whole.at[..., :cut].set(one_x.transpose(2, 1, 3, 0, 4, 5))
    whole = placed(whole, two_far, 2, 4)
    gathered = whole.reshape(model, width)

    product = jnp.dot(rows, gathered, preferred_element_type=jnp.float32)
    gate = product * scales32
    sig = jax.nn.sigmoid(gate)
    upper = up_branch.astype(jnp.float32)
    hidden = (gate * sig * upper).astype(jnp.bfloat16)
    filled = scales32 > 0.0
    dgate = jnp.where(
        filled,
        cotangent.astype(jnp.float32) * upper * sig * (1.0 + gate * (1.0 - sig)),
        0.0,
    ).astype(jnp.bfloat16)

    def pick(array, axis, which):
        return lax.dynamic_index_in_dim(array, which, axis, keepdims=False)

    def add(one, other):
        return (one.astype(jnp.float32) + other.astype(jnp.float32)).astype(jnp.bfloat16)

    partial = jnp.dot(dgate, gathered.T, preferred_element_type=jnp.float32).astype(jnp.bfloat16)
    partial = partial.reshape(2, 2, n_core, slot_count, model)

    def returned(part):
        swapped = lax.ppermute(pick(part, 2, 1 - core), "core", [(0, 1), (1, 0)])
        pair = add(pick(part, 2, core), swapped)
        near = lax.ppermute(pick(pair, 1, 1 - yl % 2), "yl", by_one)
        four = add(pick(pair, 1, yl % 2), near)
        far = lax.ppermute(pick(four, 0, 1 - yl // 2), "yl", by_two)
        return add(pick(four, 0, yl // 2), far)

    half = model // 2
    slot_grad = jnp.concatenate([returned(partial[..., :half]), returned(partial[..., half:])], axis=1)
    input_grad = jnp.einsum(
        "st,sd->td", select, slot_grad, preferred_element_type=jnp.float32
    ).astype(jnp.bfloat16)
    return (hidden, input_grad)


def solution(mesh):
    fine = Mesh(mesh.devices.reshape(SIZES), AXES)
    in_specs = (
        P(AXES, None),
        P(AXES),
        P(AXES, None),
        P(GROUP, TENSOR),
        P(GROUP, TENSOR),
        P(GROUP, TENSOR),
    )
    out_specs = (P(GROUP, TENSOR), P(AXES, None))
    return jax.shard_map(body, mesh=fine, in_specs=in_specs, out_specs=out_specs, check_vma=False)
```

```python
import jax
import jax.numpy as jnp
from jax import lax
from jax.sharding import Mesh, PartitionSpec as P

AXES = ("za", "zb", "yh", "x", "yl", "core")
SIZES = (4, 4, 2, 4, 4, 2)
GROUP = ("za", "zb", "yh", "x")
TENSOR = ("yl", "core")


def shifted(za, zb, by):
    count = za * zb
    return [(i, (i + by) % count) for i in range(count)]


def everyone(part, axes):
    count = lax.axis_size(axes)
    return lax.all_to_all(jnp.broadcast_to(part[None], (count,) + part.shape), axes, 0, 0)


def along_z(part, by):
    za, zb = lax.axis_size("za"), lax.axis_size("zb")
    return lax.ppermute(part, ("za", "zb"), shifted(za, zb, by))


def two_along_z(part):
    za, zb, core = lax.axis_size("za"), lax.axis_size("zb"), lax.axis_size("core")
    count = za * zb
    pairs = []
    for z in range(count):
        for c in range(core):
            pairs.append((z * core + c, (z + (2 if c else -2)) % count * core + c))
    return lax.ppermute(part, ("za", "zb", "core"), pairs)


def in_order(own, other, which):
    return jnp.where(which == 0, jnp.stack([own, other]), jnp.stack([other, own]))


def nothing(array):
    return (array[(0,) * array.ndim] * 0).astype(jnp.int32)


def by_residue(own, below, above, far):
    zb = lax.axis_index("zb")
    out = []
    for r in range(4):
        away = (r - zb) % 4
        out.append(
            jnp.where(away == 0, own, jnp.where(away == 1, above, jnp.where(away == 2, far, below)))
        )
    return jnp.stack(out)


def body(panel, row_scale, expert_ids, weight, up_branch, cotangent):
    n_yl, n_core = lax.axis_size("yl"), lax.axis_size("core")
    slot_count = up_branch.shape[0] // (n_yl * n_core)
    depth, width = weight.shape
    model = panel.shape[1]
    cut = (width // 2 + 127) // 128 * 128

    hit = jnp.any(expert_ids == 0, axis=1)
    place = jnp.cumsum(hit.astype(jnp.int32)) - 1
    slots = jnp.arange(slot_count, dtype=jnp.int32)
    select = ((place[None, :] == slots[:, None]) & hit[None, :]).astype(jnp.bfloat16)
    own_rows = jnp.dot(select, panel, preferred_element_type=jnp.float32).astype(jnp.bfloat16)
    own_scale = jnp.dot(
        select, jnp.broadcast_to(row_scale[:, None], (row_scale.shape[0], 128)),
        preferred_element_type=jnp.float32,
    ).astype(jnp.bfloat16)
    sent = jnp.concatenate([own_rows, own_scale], axis=1)
    core = lax.axis_index("core")

    yl = lax.axis_index("yl")
    by_one, by_two = [(i, i ^ 1) for i in range(4)], [(i, i ^ 2) for i in range(4)]
    opposite = lax.ppermute(sent, "yl", by_two)

    far = everyone(weight, ("za", "yh")).reshape(4, 2, depth, width)

    one, two = far[..., :cut], far[..., cut:]
    beside = (along_z(one, 1), along_z(one, -1), two_along_z(one))
    two_rows = in_order(sent, opposite, (yl + nothing(beside[2])) // 2)
    beyond = lax.ppermute(two_rows, "yl", by_one)
    one_x = everyone(by_residue(one, *beside), ("x",))
    two_x = everyone(two, ("x",))
    zb = lax.axis_index("zb")
    below, above = along_z(two_x, 1), along_z(two_x, -1)
    two_far = two_along_z(two_x)

    def between(even, odd):
        return jnp.concatenate([even[:1], odd[:1], even[1:], odd[1:]])

    four_rows = jnp.where(yl % 2 == 0, between(two_rows, beyond), between(beyond, two_rows))
    theirs = lax.ppermute(four_rows, "core", [(0, 1), (1, 0)])
    got = jnp.stack([four_rows, four_rows], 1)
    got = lax.dynamic_update_slice(got, theirs[:, None], (0, 1 - core, 0, 0))
    got = got.reshape(n_yl * n_core * slot_count, model + 128)
    rows = got[:, :model]
    scales32 = got[:, model:model + 1].astype(jnp.float32)

    whole = jnp.zeros((4, 4, 2, 4, depth, width), jnp.bfloat16)
    zero = jnp.zeros((), jnp.int32)

    def placed(whole, piece, by, after):
        piece = piece.transpose(1, 2, 0, 3, 4)[:, None]
        at = (zero, (zb + by + after) % 4, zero, zero, zero, zero + cut)
        return lax.dynamic_update_slice(whole, piece, at)

    whole = placed(whole, two_x, 0, 4)
    whole = placed(whole, below, -1, 4)
    whole = placed(whole, above, 1, 4)
    whole = whole.at[..., :cut].set(one_x.transpose(2, 1, 3, 0, 4, 5))
    whole = placed(whole, two_far, 2, 4)
    gathered = whole.reshape(model, width)

    product = jnp.dot(rows, gathered, preferred_element_type=jnp.float32)
    gate = product * scales32
    sig = jax.nn.sigmoid(gate)
    upper = up_branch.astype(jnp.float32)
    hidden = (gate * sig * upper).astype(jnp.bfloat16)
    filled = scales32 > 0.0
    dgate = jnp.where(
        filled,
        cotangent.astype(jnp.float32) * upper * sig * (1.0 + gate * (1.0 - sig)),
        0.0,
    ).astype(jnp.bfloat16)

    def pick(array, axis, which):
        return lax.dynamic_index_in_dim(array, which, axis, keepdims=False)

    def add(one, other):
        return (one.astype(jnp.float32) + other.astype(jnp.float32)).astype(jnp.bfloat16)

    partial = jnp.dot(dgate, gathered.T, preferred_element_type=jnp.float32).astype(jnp.bfloat16)
    partial = partial.reshape(2, 2, n_core, slot_count, model)

    def returned(part):
        swapped = lax.ppermute(pick(part, 2, 1 - core), "core", [(0, 1), (1, 0)])
        pair = add(pick(part, 2, core), swapped)
        near = lax.ppermute(pick(pair, 1, 1 - yl % 2), "yl", by_one)
        four = add(pick(pair, 1, yl % 2), near)
        far = lax.ppermute(pick(four, 0, 1 - yl // 2), "yl", by_two)
        return add(pick(four, 0, yl // 2), far)

    half = model // 2
    slot_grad = jnp.concatenate([returned(partial[..., :half]), returned(partial[..., half:])], axis=1)
    input_grad = jnp.einsum(
        "st,sd->td", select, slot_grad, preferred_element_type=jnp.float32
    ).astype(jnp.bfloat16)
    return (hidden, input_grad)


def solution(mesh):
    fine = Mesh(mesh.devices.reshape(SIZES), AXES)
    in_specs = (
        P(AXES, None),
        P(AXES),
        P(AXES, None),
        P(GROUP, TENSOR),
        P(GROUP, TENSOR),
        P(GROUP, TENSOR),
    )
    out_specs = (P(GROUP, TENSOR), P(AXES, None))
    return jax.shard_map(body, mesh=fine, in_specs=in_specs, out_specs=out_specs, check_vma=False)
```

```python
import jax
import jax.numpy as jnp
from jax import lax
from jax.sharding import Mesh, PartitionSpec as P

AXES = ("za", "zb", "yh", "x", "yl", "core")
SIZES = (4, 4, 2, 4, 4, 2)
GROUP = ("za", "zb", "yh", "x")
TENSOR = ("yl", "core")


def shifted(za, zb, by):
    count = za * zb
    return [(i, (i + by) % count) for i in range(count)]


def everyone(part, axes):
    count = lax.axis_size(axes)
    return lax.all_to_all(jnp.broadcast_to(part[None], (count,) + part.shape), axes, 0, 0)


def along_z(part, by):
    za, zb = lax.axis_size("za"), lax.axis_size("zb")
    return lax.ppermute(part, ("za", "zb"), shifted(za, zb, by))


def two_along_z(part):
    za, zb, core = lax.axis_size("za"), lax.axis_size("zb"), lax.axis_size("core")
    count = za * zb
    pairs = []
    for z in range(count):
        for c in range(core):
            pairs.append((z * core + c, (z + (2 if c else -2)) % count * core + c))
    return lax.ppermute(part, ("za", "zb", "core"), pairs)


def in_order(own, other, which):
    return jnp.where(which == 0, jnp.stack([own, other]), jnp.stack([other, own]))


def nothing(array):
    return (array[(0,) * array.ndim] * 0).astype(jnp.int32)


def by_residue(own, below, above, far):
    zb = lax.axis_index("zb")
    out = []
    for r in range(4):
        away = (r - zb) % 4
        out.append(
            jnp.where(away == 0, own, jnp.where(away == 1, above, jnp.where(away == 2, far, below)))
        )
    return jnp.stack(out)


def body(panel, row_scale, expert_ids, weight, up_branch, cotangent):
    n_yl, n_core = lax.axis_size("yl"), lax.axis_size("core")
    slot_count = up_branch.shape[0] // (n_yl * n_core)
    depth, width = weight.shape
    model = panel.shape[1]
    cut = (width // 2 + 127) // 128 * 128

    hit = jnp.any(expert_ids == 0, axis=1)
    place = jnp.cumsum(hit.astype(jnp.int32)) - 1
    slots = jnp.arange(slot_count, dtype=jnp.int32)
    select = ((place[None, :] == slots[:, None]) & hit[None, :]).astype(jnp.bfloat16)
    own_rows = jnp.dot(select, panel, preferred_element_type=jnp.float32).astype(jnp.bfloat16)
    own_scale = jnp.dot(
        select, jnp.broadcast_to(row_scale[:, None], (row_scale.shape[0], 128)),
        preferred_element_type=jnp.float32,
    ).astype(jnp.bfloat16)
    sent = jnp.concatenate([own_rows, own_scale], axis=1)
    core = lax.axis_index("core")

    yl = lax.axis_index("yl")
    by_one, by_two = [(i, i ^ 1) for i in range(4)], [(i, i ^ 2) for i in range(4)]
    opposite = lax.ppermute(sent, "yl", by_two)

    far = everyone(weight, ("za", "yh")).reshape(4, 2, depth, width)

    one, two = far[..., :cut], far[..., cut:]
    beside = (along_z(one, 1), along_z(one, -1), two_along_z(one))
    two_rows = in_order(sent, opposite, (yl + nothing(beside[2])) // 2)
    beyond = lax.ppermute(two_rows, "yl", by_one)
    one_x = everyone(by_residue(one, *beside), ("x",))
    two_x = everyone(two, ("x",))
    zb = lax.axis_index("zb")
    below, above = along_z(two_x, 1), along_z(two_x, -1)
    two_far = two_along_z(two_x)

    def between(even, odd):
        return jnp.concatenate([even[:1], odd[:1], even[1:], odd[1:]])

    four_rows = jnp.where(yl % 2 == 0, between(two_rows, beyond), between(beyond, two_rows))
    theirs = lax.ppermute(four_rows, "core", [(0, 1), (1, 0)])
    got = jnp.zeros((n_yl, n_core) + four_rows.shape[1:], four_rows.dtype)
    got = lax.dynamic_update_slice(got, four_rows[:, None], (0, core, 0, 0))
    got = lax.dynamic_update_slice(got, theirs[:, None], (0, 1 - core, 0, 0))
    got = got.reshape(n_yl * n_core * slot_count, model + 128)
    rows = got[:, :model]
    scales32 = got[:, model:model + 1].astype(jnp.float32)

    whole = jnp.zeros((4, 4, 2, 4, depth, width), jnp.bfloat16)
    zero = jnp.zeros((), jnp.int32)

    def placed(whole, piece, by, after):
        piece = piece.transpose(1, 2, 0, 3, 4)[:, None]
        at = (zero, (zb + by + after) % 4, zero, zero, zero, zero + cut)
        return lax.dynamic_update_slice(whole, piece, at)

    whole = placed(whole, two_x, 0, 4)
    whole = placed(whole, below, -1, 4)
    whole = placed(whole, above, 1, 4)
    whole = whole.at[..., :cut].set(one_x.transpose(2, 1, 3, 0, 4, 5))
    whole = placed(whole, two_far, 2, 4)
    gathered = whole.reshape(model, width)

    product = jnp.dot(rows, gathered, preferred_element_type=jnp.float32)
    gate = product * scales32
    sig = jax.nn.sigmoid(gate)
    upper = up_branch.astype(jnp.float32)
    hidden = (gate * sig * upper).astype(jnp.bfloat16)
    filled = scales32 > 0.0
    dgate = jnp.where(
        filled,
        cotangent.astype(jnp.float32) * upper * sig * (1.0 + gate * (1.0 - sig)),
        0.0,
    ).astype(jnp.bfloat16)

    def pick(array, axis, which):
        return lax.dynamic_index_in_dim(array, which, axis, keepdims=False)

    def add(one, other):
        return (one.astype(jnp.float32) + other.astype(jnp.float32)).astype(jnp.bfloat16)

    partial = jnp.dot(dgate, gathered.T, preferred_element_type=jnp.float32).astype(jnp.bfloat16)
    partial = partial.reshape(2, 2, n_core, slot_count, model)

    def returned(part):
        swapped = lax.ppermute(pick(part, 2, 1 - core), "core", [(0, 1), (1, 0)])
        pair = add(pick(part, 2, core), swapped)
        near = lax.ppermute(pick(pair, 1, 1 - yl % 2), "yl", by_one)
        four = add(pick(pair, 1, yl % 2), near)
        far = lax.ppermute(pick(four, 0, 1 - yl // 2), "yl", by_two)
        return add(pick(four, 0, yl // 2), far)

    half = model // 2
    slot_grad = jnp.concatenate([returned(partial[..., :half]), returned(partial[..., half:])], axis=1)
    input_grad = jnp.einsum(
        "st,sd->td", select, slot_grad, preferred_element_type=jnp.float32
    ).astype(jnp.bfloat16)
    return (hidden, input_grad)


def solution(mesh):
    fine = Mesh(mesh.devices.reshape(SIZES), AXES)
    in_specs = (
        P(AXES, None),
        P(AXES),
        P(AXES, None),
        P(GROUP, TENSOR),
        P(GROUP, TENSOR),
        P(GROUP, TENSOR),
    )
    out_specs = (P(GROUP, TENSOR), P(AXES, None))
    return jax.shard_map(body, mesh=fine, in_specs=in_specs, out_specs=out_specs, check_vma=False)
```
